32 devices in a mesh: gx: 4 (over y, x), gy: 8 (over z, core).
Axes of the slice: x: 2, y: 2, z: 4, core: 2. Of those that a mesh axis runs over, the one named last changes fastest.
Arguments:
- energy: float32 [64, 1024, 128], P('gx', 'gy'), may hold values from 1 to 5
- coupling: float32 [64, 1024, 128], P('gx', 'gy'), may hold values from 4000 to 40000
Outputs:
- energy_next: float32 [64, 1024, 128], P('gx', 'gy')
The draws below stay inside these ranges and needn't reach their ends.
All inputs are finite; a program needn't handle non-finite values.
Results may differ from the reference program's by a relative error of at most 0.0003.
Values sent between devices are 32-bit elements; how exact they have to be, the bound alone decides.
A program may use at most 64 MiB of HBM per device.

```python
import math
import jax
import jax.numpy as jnp
from jax import lax

NZ = 128
NX = 64
NY = 1024


def levels(rng, extent, shards, least, largest):
    def one(dim, blocks):
        heights = jax.random.uniform(jax.random.fold_in(jax.random.fold_in(rng, 6), dim), (blocks,), jnp.float32, least / len(shards), largest / len(shards))
        return jnp.repeat(jnp.exp(heights), extent[dim] // blocks).reshape((-1,) + (1,) * (len(extent) - dim - 1))

    gain = one(*shards[0])
    for cut in shards[1:]:
        gain = gain * one(*cut)
    return gain


def setup_inputs(seed: int = 0) -> dict:
    key_list = jax.random.split(jax.random.key(seed), 3)
    energy = jnp.clip(1.0 + 4.0 * jax.random.uniform(key_list[0], (NX, NY, NZ), jnp.float32) ** levels(key_list[0], (NX, NY, NZ), ((0, 4), (1, 8)), -0.2, 0.2), 1.0, 5.0)
    coupling = jnp.clip(jnp.exp(math.log(40000.0) - 2.3025851 * jax.random.uniform(key_list[1], (NX, NY, NZ), jnp.float32) ** levels(key_list[1], (NX, NY, NZ), ((0, 4), (1, 8)), -0.2, 0.2)), 4000.0, 40000.0)
    return {"energy": energy, "coupling": coupling}


y_weight = 0.15


def line_solve(diag_part, lower_part, upper_part, sources):
    def forward(running, row):
        prev_ratio, prev_value = running
        diag_row, lower_row, upper_row, source_row = row
        denom = diag_row - lower_row * prev_ratio
        new_ratio = upper_row / denom
        new_value = (source_row - lower_row * prev_value) / denom
        return (new_ratio, new_value), (new_ratio, new_value)

    start = (jnp.zeros(diag_part.shape[1:], jnp.float32), jnp.zeros(diag_part.shape[1:], jnp.float32))
    _, (ratios, values) = lax.scan(forward, start, (diag_part, lower_part, upper_part, sources))

    def backward(later_value, row):
        ratio_row, value_row = row
        result = value_row - ratio_row * later_value
        return result, result

    _, solved = lax.scan(backward, jnp.zeros(diag_part.shape[1:], jnp.float32), (ratios, values), reverse=True)
    return solved


def reference(energy, coupling):
    padded = jnp.pad(energy, ((0, 0), (1, 1), (0, 0)))
    source_term = energy + y_weight * (padded[:, :-2] - 2.0 * energy + padded[:, 2:])
    right_face = jnp.concatenate([coupling[1:], jnp.zeros_like(coupling[:1])], 0)
    diag_part = 1.0 + coupling + right_face
    return line_solve(diag_part, -coupling, -right_face, source_term)
```

```python
import functools

import jax
import jax.numpy as jnp
from jax import lax
from jax.experimental import pallas as pl
from jax.experimental.pallas import tpu as pltpu
from jax.sharding import PartitionSpec as P

Y_WEIGHT = 0.15
CHUNKS = 4
LAG = 2
PAD = 8
MESH = pl.DeviceIdType.MESH


def kernel(
    gx_size, gy_size, chunks, lag,
    energy_ref, coupling_ref, out_ref,
    e_v, c_v, b_v, r_v, g_v, edge, halo, outbox, inbox, usend, ubox,
    load_sem, face_sem, halo_send, halo_recv, msg_send, msg_recv, u_send, u_recv,
):
    height, width, _ = energy_ref.shape
    size = width // chunks
    p, q = lax.axis_index("gx"), lax.axis_index("gy")
    half = gx_size // 2
    is_left = p < half
    is_right = p >= half
    is_end = (p == 0) | (p == gx_size - 1)
    is_mid = (p == half - 1) | (p == half)
    not_end = jnp.logical_not(is_end)
    not_mid = jnp.logical_not(is_mid)
    inward = jnp.where(is_left, p + 1, p - 1)
    outward = jnp.where(is_left, p - 1, p + 1)
    slot = jnp.where(is_mid, 1, 0)
    order = list(range(1, chunks - 1)) + [0, chunks - 1] if chunks > 2 else list(range(chunks))

    barrier = pltpu.get_barrier_semaphore()
    has_down, has_up = q > 0, q < gy_size - 1

    def greet(cond, device):
        @pl.when(cond)
        def _():
            pl.semaphore_signal(barrier, inc=1, device_id=device, device_id_type=MESH)

    greet(p > 0, (p - 1, q))
    greet(p < gx_size - 1, (p + 1, q))
    greet(has_down, (p, q - 1))
    greet(has_up, (p, q + 1))

    load = pltpu.make_async_copy(energy_ref, e_v.at[:, PAD:PAD + width, :], load_sem)
    load.start()

    def face_load(k):
        cut = pl.ds(k * size, size)
        return pltpu.make_async_copy(coupling_ref.at[:, cut, :], c_v.at[:, cut, :], face_sem.at[k])

    for k in order:
        face_load(k).start()

    @pl.when(is_end)
    def _():
        inbox[0, :, 0] = jnp.zeros_like(inbox[0, :, 0])
        inbox[0, :, 1] = jnp.zeros_like(inbox[0, :, 1])

    load.wait()
    for i in range(height):
        edge[0, i:i + 1, :] = e_v[i, PAD:PAD + 1, :]
        edge[1, i:i + 1, :] = e_v[i, PAD + width - 1:PAD + width, :]

    @pl.when(jnp.logical_not(has_down))
    def _():
        halo[0] = jnp.zeros_like(halo[0])

    @pl.when(jnp.logical_not(has_up))
    def _():
        halo[1] = jnp.zeros_like(halo[1])

    count = (
        jnp.where(p > 0, 1, 0) + jnp.where(p < gx_size - 1, 1, 0)
        + jnp.where(has_down, 1, 0) + jnp.where(has_up, 1, 0)
    )
    pl.semaphore_wait(barrier, count)

    def halo_copy(side, device):
        return pltpu.make_async_remote_copy(
            src_ref=edge.at[side], dst_ref=halo.at[1 - side],
            send_sem=halo_send.at[side], recv_sem=halo_recv.at[1 - side],
            device_id=device, device_id_type=MESH,
        )

    to_down = halo_copy(0, (p, q - 1))
    to_up = halo_copy(1, (p, q + 1))

    @pl.when(has_down)
    def _():
        to_down.start()

    @pl.when(has_up)
    def _():
        to_up.start()

    def wait_halo(k):
        if k == 0:
            @pl.when(has_down)
            def _():
                to_up.wait_recv()

            for i in range(height):
                e_v[i, PAD - 1:PAD, :] = halo[0, i:i + 1, :]
        if k == chunks - 1:
            @pl.when(has_up)
            def _():
                to_down.wait_recv()

            for i in range(height):
                e_v[i, PAD + width:PAD + width + 1, :] = halo[1, i:i + 1, :]

    def make_source(k):
        wait_halo(k)
        at = k * size

        def row(i, carry):
            here = e_v[i, PAD + at:PAD + at + size, :]
            before = e_v[i, PAD + at - 1:PAD + at + size - 1, :]
            after = e_v[i, PAD + at + 1:PAD + at + size + 1, :]
            b_v[i, at:at + size, :] = here + Y_WEIGHT * (before - 2.0 * here + after)
            return carry

        lax.fori_loop(0, height, row, 0, unroll=True)

    def message(k):
        return pltpu.make_async_remote_copy(
            src_ref=outbox.at[k], dst_ref=inbox.at[slot, k],
            send_sem=msg_send.at[k], recv_sem=msg_recv.at[slot, k],
            device_id=(inward, q), device_id_type=MESH,
        )

    def arrival(s, k):
        return pltpu.make_async_remote_copy(
            src_ref=outbox.at[k], dst_ref=inbox.at[s, k],
            send_sem=msg_send.at[k], recv_sem=msg_recv.at[s, k],
            device_id=(inward, q), device_id_type=MESH,
        )

    def reply(k):
        return pltpu.make_async_remote_copy(
            src_ref=usend.at[k], dst_ref=ubox.at[k],
            send_sem=u_send.at[k], recv_sem=u_recv.at[k],
            device_id=(outward, q), device_id_type=MESH,
        )

    def eliminate(k):
        rows = slice(k * size, (k + 1) * size)

        @pl.when(is_left)
        def _():
            e, f = inbox[0, k, 0], inbox[0, k, 1]
            c = c_v[0, rows, :]
            g = 1.0 / (c + e)
            r = c * g
            r_v[0, rows, :] = r
            g_v[0, rows, :] = g * f
            e = 1.0 + jnp.where(p == 0, c, r * e)
            f = b_v[0, rows, :] + r * f

            def step(i, carry):
                e, f = carry
                c = c_v[i, rows, :]
                g = 1.0 / (c + e)
                r = c * g
                r_v[i, rows, :] = r
                g_v[i, rows, :] = g * f
                return 1.0 + r * e, b_v[i, rows, :] + r * f

            e, f = lax.fori_loop(1, height, step, (e, f), unroll=True)
            outbox[k, 0] = e
            outbox[k, 1] = f

        @pl.when(is_right)
        def _():
            def step(t, carry):
                e, f = carry
                i = height - 1 - t
                e = 1.0 + e
                f = b_v[i, rows, :] + f
                c = c_v[i, rows, :]
                g = 1.0 / (c + e)
                r = c * g
                r_v[i, rows, :] = r
                g_v[i, rows, :] = g * f
                return r * e, r * f

            e, f = lax.fori_loop(0, height, step, (inbox[0, k, 0], inbox[0, k, 1]), unroll=True)
            outbox[k, 0] = e
            outbox[k, 1] = f

    def substitute(k):
        rows = slice(k * size, (k + 1) * size)

        @pl.when(is_left)
        def _():
            u = ubox[k]
            out_ref[height - 1, rows, :] = u

            def step(t, u):
                i = height - 1 - t
                u = g_v[i, rows, :] + r_v[i, rows, :] * u
                out_ref[i - 1, rows, :] = u
                return u

            u = lax.fori_loop(0, height - 1, step, u, unroll=True)
            usend[k] = g_v[0, rows, :] + r_v[0, rows, :] * u

        @pl.when(is_right)
        def _():
            def step(i, u):
                u = g_v[i, rows, :] + r_v[i, rows, :] * u
                out_ref[i, rows, :] = u
                return u

            usend[k] = lax.fori_loop(0, height, step, ubox[k], unroll=True)

    @pl.when(not_end)
    def _():
        for k in order:
            make_source(k)

    for step in range(chunks + lag):
        if step < chunks:
            k = order[step]
            face_load(k).wait()

            @pl.when(is_end)
            def _():
                make_source(k)

            @pl.when(not_end)
            def _():
                arrival(0, k).wait_recv()

            eliminate(k)
            message(k).start()
        if step >= lag:
            k = order[step - lag]

            @pl.when(is_mid)
            def _():
                arrival(1, k).wait_recv()
                ubox[k] = (outbox[k, 1] + inbox[1, k, 1]) / (outbox[k, 0] + inbox[1, k, 0])

            @pl.when(not_mid)
            def _():
                reply(k).wait_recv()

            substitute(k)

            @pl.when(not_end)
            def _():
                reply(k).start()

    for k in order:
        message(k).wait_send()

        @pl.when(not_end)
        def _():
            reply(k).wait_send()

    @pl.when(has_down)
    def _():
        to_down.wait_send()

    @pl.when(has_up)
    def _():
        to_up.wait_send()


def body(energy, coupling):
    height, width, depth = energy.shape
    gx_size, gy_size = lax.axis_size("gx"), lax.axis_size("gy")
    size = width // CHUNKS
    f32 = jnp.float32
    block = pltpu.VMEM((height, width, depth), f32)
    dma = pltpu.SemaphoreType.DMA
    return pl.pallas_call(
        functools.partial(kernel, gx_size, gy_size, CHUNKS, LAG),
        out_shape=jax.ShapeDtypeStruct(energy.shape, f32),
        in_specs=[pl.BlockSpec(memory_space=pl.ANY)] * 2,
        out_specs=pl.BlockSpec(memory_space=pltpu.VMEM),
        scratch_shapes=[
            pltpu.VMEM((height, width + 2 * PAD, depth), f32),
            block, block, block, block,
            pltpu.VMEM((2, height, depth), f32),
            pltpu.VMEM((2, height, depth), f32),
            pltpu.VMEM((CHUNKS, 2, size, depth), f32),
            pltpu.VMEM((2, CHUNKS, 2, size, depth), f32),
            pltpu.VMEM((CHUNKS, size, depth), f32),
            pltpu.VMEM((CHUNKS, size, depth), f32),
            dma, dma((CHUNKS,)), dma((2,)), dma((2,)),
            dma((CHUNKS,)), dma((2, CHUNKS)), dma((CHUNKS,)), dma((CHUNKS,)),
        ],
        compiler_params=pltpu.CompilerParams(
            collective_id=0, has_side_effects=True, vmem_limit_bytes=32 * 1024 * 1024
        ),
        cost_estimate=pl.CostEstimate(
            flops=30 * height * width * depth, bytes_accessed=12 * height * width * depth, transcendentals=0
        ),
    )(energy, coupling)


def solution(mesh):
    spec = P("gx", "gy", None)
    return jax.shard_map(body, mesh=mesh, in_specs=(spec, spec), out_specs=spec, check_vma=False)
```

```python
import functools

import jax
import jax.numpy as jnp
from jax import lax
from jax.experimental import pallas as pl
from jax.experimental.pallas import tpu as pltpu
from jax.sharding import PartitionSpec as P

Y_WEIGHT = 0.15
PIECES = 4
PAD = 8
VMEM_LIMIT = 52 * 1024 * 1024
MESH = pl.DeviceIdType.MESH


def chunk_list(width):
    tiles = width // PAD - 2
    cuts = [2 * PAD + PAD * (tiles * n // PIECES) for n in range(PIECES + 1)]
    return [(a, b - a) for a, b in zip(cuts, cuts[1:])] + [(0, 2 * PAD)]


def kernel(
    gx_size, gy_size, energy_ref, coupling_ref, out_ref,
    e_v, c_v, b_v, r_v, g_v, edge, halo, outbox, inbox, usend, ubox,
    load_sem, face_sem, halo_send, halo_recv, msg_send, msg_recv, u_send, u_recv,
):
    height, width, _ = energy_ref.shape
    chunks = chunk_list(width)
    count = len(chunks)
    p, q = lax.axis_index("gx"), lax.axis_index("gy")
    half = gx_size // 2
    is_left = p < half
    is_right = p >= half
    is_end = (p == 0) | (p == gx_size - 1)
    is_mid = (p == half - 1) | (p == half)
    not_end = jnp.logical_not(is_end)
    not_mid = jnp.logical_not(is_mid)
    inward = jnp.where(is_left, p + 1, p - 1)
    outward = jnp.where(is_left, p - 1, p + 1)
    slot = jnp.where(is_mid, 1, 0)
    has_down, has_up = q > 0, q < gy_size - 1

    def segments(k):
        start, size = chunks[k]
        if start == 0:
            return [(0, width - PAD, PAD), (PAD, 0, PAD)]
        return [(0, start - PAD, size)]

    def take(ref, i, k, shift=0):
        parts = [ref[i, line + shift:line + shift + n, :] for _, line, n in segments(k)]
        return parts[0] if len(parts) == 1 else jnp.concatenate(parts, axis=0)

    def put(ref, i, k, value):
        for at, line, n in segments(k):
            ref[i, line:line + n, :] = value[at:at + n]

    def rows(k):
        start, size = chunks[k]
        return slice(start, start + size)

    barrier = pltpu.get_barrier_semaphore()

    def greet(cond, device):
        @pl.when(cond)
        def _():
            pl.semaphore_signal(barrier, inc=1, device_id=device, device_id_type=MESH)

    greet(p > 0, (p - 1, q))
    greet(p < gx_size - 1, (p + 1, q))
    greet(has_down, (p, q - 1))
    greet(has_up, (p, q + 1))

    load = pltpu.make_async_copy(energy_ref, e_v.at[:, PAD:PAD + width, :], load_sem)
    load.start()
    face_load = pltpu.make_async_copy(coupling_ref, c_v, face_sem)
    face_load.start()

    @pl.when(is_end)
    def _():
        inbox[0] = jnp.zeros_like(inbox[0])

    load.wait()
    for i in range(height):
        edge[0, i:i + 1, :] = e_v[i, PAD:PAD + 1, :]
        edge[1, i:i + 1, :] = e_v[i, PAD + width - 1:PAD + width, :]

    @pl.when(jnp.logical_not(has_down))
    def _():
        halo[0] = jnp.zeros_like(halo[0])

    @pl.when(jnp.logical_not(has_up))
    def _():
        halo[1] = jnp.zeros_like(halo[1])

    def halo_copy(side, device):
        return pltpu.make_async_remote_copy(
            src_ref=edge.at[side], dst_ref=halo.at[1 - side],
            send_sem=halo_send.at[side], recv_sem=halo_recv.at[1 - side],
            device_id=device, device_id_type=MESH,
        )

    to_down = halo_copy(0, (p, q - 1))
    to_up = halo_copy(1, (p, q + 1))

    def make_source(k):
        def row(i, carry):
            here, before, after = take(e_v, i, k, PAD), take(e_v, i, k, PAD - 1), take(e_v, i, k, PAD + 1)
            b_v[i, rows(k), :] = here + Y_WEIGHT * (before - 2.0 * here + after)
            return carry

        lax.fori_loop(0, height, row, 0, unroll=True)

    def message(s, k):
        return pltpu.make_async_remote_copy(
            src_ref=outbox.at[:, rows(k), :], dst_ref=inbox.at[s, :, rows(k), :],
            send_sem=msg_send.at[k], recv_sem=msg_recv.at[s, k],
            device_id=(inward, q), device_id_type=MESH,
        )

    def reply(k):
        return pltpu.make_async_remote_copy(
            src_ref=usend.at[rows(k)], dst_ref=ubox.at[rows(k)],
            send_sem=u_send.at[k], recv_sem=u_recv.at[k],
            device_id=(outward, q), device_id_type=MESH,
        )

    def eliminate(k):
        at = rows(k)

        @pl.when(is_left)
        def _():
            def step(i, carry):
                e, f = carry
                c = take(c_v, i, k)
                g = 1.0 / (c + e)
                r = c * g
                r_v[i, at, :] = r
                g_v[i, at, :] = g * f
                through = r * e
                if isinstance(i, int):
                    through = jnp.where(p == 0, c, through)
                return 1.0 + through, b_v[i, at, :] + r * f

            carry = step(0, (inbox[0, 0, at, :], inbox[0, 1, at, :]))
            e, f = lax.fori_loop(1, height, step, carry, unroll=True)
            outbox[0, at, :] = e
            outbox[1, at, :] = f

        @pl.when(is_right)
        def _():
            def step(t, carry):
                e, f = carry
                i = height - 1 - t
                e = 1.0 + e
                f = b_v[i, at, :] + f
                c = take(c_v, i, k)
                g = 1.0 / (c + e)
                r = c * g
                r_v[i, at, :] = r
                g_v[i, at, :] = g * f
                return r * e, r * f

            carry = (inbox[0, 0, at, :], inbox[0, 1, at, :])
            e, f = lax.fori_loop(0, height, step, carry, unroll=True)
            outbox[0, at, :] = e
            outbox[1, at, :] = f

    def prepare(k):
        at = rows(k)

        def step(t, carry):
            a, b = carry
            i = jnp.where(is_left, height - 1 - t, t)
            r = r_v[i, at, :]
            a = g_v[i, at, :] + r * a
            b = r * b
            g_v[i, at, :] = a
            r_v[i, at, :] = b
            return a, b

        first = jnp.where(is_left, height - 1, 0)
        lax.fori_loop(1, height, step, (g_v[first, at, :], r_v[first, at, :]), unroll=True)

    def substitute(k):
        at = rows(k)

        @pl.when(is_left)
        def _():
            u = ubox[at, :]
            put(out_ref, height - 1, k, u)

            def step(i, carry):
                put(out_ref, i - 1, k, g_v[i, at, :] + r_v[i, at, :] * u)
                return carry

            lax.fori_loop(1, height, step, 0, unroll=True)

        @pl.when(is_right)
        def _():
            u = ubox[at, :]

            def step(i, carry):
                put(out_ref, i, k, g_v[i, at, :] + r_v[i, at, :] * u)
                return carry

            lax.fori_loop(0, height, step, 0, unroll=True)

    for k in range(count - 1):
        make_source(k)
    face_load.wait()
    greeted = (
        jnp.where(p > 0, 1, 0) + jnp.where(p < gx_size - 1, 1, 0)
        + jnp.where(has_down, 1, 0) + jnp.where(has_up, 1, 0)
    )

    @pl.when(is_end)
    def _():
        eliminate(0)

    pl.semaphore_wait(barrier, greeted)

    @pl.when(has_down)
    def _():
        to_down.start()

    @pl.when(has_up)
    def _():
        to_up.start()

    for k in range(count):
        if k == count - 1:
            @pl.when(has_down)
            def _():
                to_up.wait_recv()

            @pl.when(has_up)
            def _():
                to_down.wait_recv()

            for i in range(height):
                e_v[i, PAD - 1:PAD, :] = halo[0, i:i + 1, :]
                e_v[i, PAD + width:PAD + width + 1, :] = halo[1, i:i + 1, :]
            make_source(k)

        @pl.when(not_end)
        def _():
            message(0, k).wait_recv()
            if k == 0:
                eliminate(k)

        if k > 0:
            eliminate(k)
        message(slot, k).start()
        prepare(k)

    last = jnp.where(is_left, 0, height - 1)
    for k in range(count):
        at = rows(k)

        @pl.when(is_mid)
        def _():
            message(1, k).wait_recv()
            ubox[at, :] = (outbox[1, at, :] + inbox[1, 1, at, :]) / (outbox[0, at, :] + inbox[1, 0, at, :])

        @pl.when(not_mid)
        def _():
            reply(k).wait_recv()

        @pl.when(not_end)
        def _():
            usend[at, :] = g_v[last, at, :] + r_v[last, at, :] * ubox[at, :]
            reply(k).start()

        substitute(k)

    for k in range(count):
        message(slot, k).wait_send()

        @pl.when(not_end)
        def _():
            reply(k).wait_send()

    @pl.when(has_down)
    def _():
        to_down.wait_send()

    @pl.when(has_up)
    def _():
        to_up.wait_send()


def body(energy, coupling):
    height, width, depth = energy.shape
    gx_size, gy_size = lax.axis_size("gx"), lax.axis_size("gy")
    count = len(chunk_list(width))
    f32 = jnp.float32
    block = pltpu.VMEM((height, width, depth), f32)
    plane = pltpu.VMEM((width, depth), f32)
    dma = pltpu.SemaphoreType.DMA
    return pl.pallas_call(
        functools.partial(kernel, gx_size, gy_size),
        out_shape=jax.ShapeDtypeStruct(energy.shape, f32),
        in_specs=[pl.BlockSpec(memory_space=pl.ANY)] * 2,
        out_specs=pl.BlockSpec(memory_space=pltpu.VMEM),
        scratch_shapes=[
            pltpu.VMEM((height, width + 2 * PAD, depth), f32),
            block, block, block, block,
            pltpu.VMEM((2, height, depth), f32),
            pltpu.VMEM((2, height, depth), f32),
            pltpu.VMEM((2, width, depth), f32),
            pltpu.VMEM((2, 2, width, depth), f32),
            plane, plane,
            dma, dma, dma((2,)), dma((2,)),
            dma((count,)), dma((2, count)), dma((count,)), dma((count,)),
        ],
        compiler_params=pltpu.CompilerParams(
            collective_id=0, has_side_effects=True, vmem_limit_bytes=VMEM_LIMIT
        ),
        cost_estimate=pl.CostEstimate(
            flops=30 * height * width * depth, bytes_accessed=12 * height * width * depth, transcendentals=0
        ),
    )(energy, coupling)


def solution(mesh):
    spec = P("gx", "gy", None)
    return jax.shard_map(body, mesh=mesh, in_specs=(spec, spec), out_specs=spec, check_vma=False)
```

```python
import functools

import jax
import jax.numpy as jnp
from jax import lax
from jax.experimental import pallas as pl
from jax.experimental.pallas import tpu as pltpu
from jax.sharding import PartitionSpec as P

Y_WEIGHT = 0.15
PIECES = 7
PAD = 8
VMEM_LIMIT = 52 * 1024 * 1024
MESH = pl.DeviceIdType.MESH


def chunk_list(width):
    tiles = width // PAD - 2
    cuts = [2 * PAD + PAD * (tiles * n // PIECES) for n in range(PIECES + 1)]
    return [(a, b - a) for a, b in zip(cuts, cuts[1:])] + [(0, 2 * PAD)]


def kernel(
    gx_size, gy_size, energy_ref, coupling_ref, out_ref,
    e_v, c_v, b_v, r_v, g_v, edge, halo, outbox, inbox, usend, ubox,
    load_sem, face_sem, halo_send, halo_recv, msg_send, msg_recv, u_send, u_recv,
):
    height, width, _ = energy_ref.shape
    chunks = chunk_list(width)
    count = len(chunks)
    p, q = lax.axis_index("gx"), lax.axis_index("gy")
    half = gx_size // 2
    is_left = p < half
    is_right = p >= half
    is_end = (p == 0) | (p == gx_size - 1)
    is_mid = (p == half - 1) | (p == half)
    not_end = jnp.logical_not(is_end)
    not_mid = jnp.logical_not(is_mid)
    inward = jnp.where(is_left, p + 1, p - 1)
    outward = jnp.where(is_left, p - 1, p + 1)
    slot = jnp.where(is_mid, 1, 0)
    has_down, has_up = q > 0, q < gy_size - 1

    def segments(k):
        start, size = chunks[k]
        if start == 0:
            return [(0, width - PAD, PAD), (PAD, 0, PAD)]
        return [(0, start - PAD, size)]

    def take(ref, i, k, shift=0):
        parts = [ref[i, line + shift:line + shift + n, :] for _, line, n in segments(k)]
        return parts[0] if len(parts) == 1 else jnp.concatenate(parts, axis=0)

    def put(ref, i, k, value):
        for at, line, n in segments(k):
            ref[i, line:line + n, :] = value[at:at + n]

    def rows(k):
        start, size = chunks[k]
        return slice(start, start + size)

    barrier = pltpu.get_barrier_semaphore()

    def greet(cond, device):
        @pl.when(cond)
        def _():
            pl.semaphore_signal(barrier, inc=1, device_id=device, device_id_type=MESH)

    greet(p > 0, (p - 1, q))
    greet(p < gx_size - 1, (p + 1, q))
    greet(has_down, (p, q - 1))
    greet(has_up, (p, q + 1))

    load = pltpu.make_async_copy(energy_ref, e_v.at[:, PAD:PAD + width, :], load_sem)
    load.start()
    face_load = pltpu.make_async_copy(coupling_ref, c_v, face_sem)
    face_load.start()

    @pl.when(is_end)
    def _():
        inbox[0] = jnp.zeros_like(inbox[0])

    load.wait()
    for i in range(height):
        edge[0, i:i + 1, :] = e_v[i, PAD:PAD + 1, :]
        edge[1, i:i + 1, :] = e_v[i, PAD + width - 1:PAD + width, :]

    @pl.when(jnp.logical_not(has_down))
    def _():
        halo[0] = jnp.zeros_like(halo[0])

    @pl.when(jnp.logical_not(has_up))
    def _():
        halo[1] = jnp.zeros_like(halo[1])

    def halo_copy(side, device):
        return pltpu.make_async_remote_copy(
            src_ref=edge.at[side], dst_ref=halo.at[1 - side],
            send_sem=halo_send.at[side], recv_sem=halo_recv.at[1 - side],
            device_id=device, device_id_type=MESH,
        )

    to_down = halo_copy(0, (p, q - 1))
    to_up = halo_copy(1, (p, q + 1))

    def make_source(k):
        def row(i, carry):
            here, before, after = take(e_v, i, k, PAD), take(e_v, i, k, PAD - 1), take(e_v, i, k, PAD + 1)
            b_v[i, rows(k), :] = here + Y_WEIGHT * (before - 2.0 * here + after)
            return carry

        lax.fori_loop(0, height, row, 0, unroll=True)

    def message(s, k):
        return pltpu.make_async_remote_copy(
            src_ref=outbox.at[:, rows(k), :], dst_ref=inbox.at[s, :, rows(k), :],
            send_sem=msg_send.at[k], recv_sem=msg_recv.at[s, k],
            device_id=(inward, q), device_id_type=MESH,
        )

    def reply(k):
        return pltpu.make_async_remote_copy(
            src_ref=usend.at[rows(k)], dst_ref=ubox.at[rows(k)],
            send_sem=u_send.at[k], recv_sem=u_recv.at[k],
            device_id=(outward, q), device_id_type=MESH,
        )

    def eliminate(k):
        at = rows(k)

        @pl.when(is_left)
        def _():
            def step(i, carry):
                e, f = carry
                c = take(c_v, i, k)
                g = pl.reciprocal(c + e)
                r = c * g
                r_v[i, at, :] = r
                g_v[i, at, :] = g * f
                through = r * e
                if isinstance(i, int):
                    through = jnp.where(p == 0, c, through)
                return 1.0 + through, b_v[i, at, :] + r * f

            carry = step(0, (inbox[0, 0, at, :], inbox[0, 1, at, :]))
            e, f = lax.fori_loop(1, height, step, carry, unroll=True)
            outbox[0, at, :] = e
            outbox[1, at, :] = f

        @pl.when(is_right)
        def _():
            def step(t, carry):
                e, f = carry
                i = height - 1 - t
                e = 1.0 + e
                f = b_v[i, at, :] + f
                c = take(c_v, i, k)
                g = pl.reciprocal(c + e)
                r = c * g
                r_v[i, at, :] = r
                g_v[i, at, :] = g * f
                return r * e, r * f

            carry = (inbox[0, 0, at, :], inbox[0, 1, at, :])
            e, f = lax.fori_loop(0, height, step, carry, unroll=True)
            outbox[0, at, :] = e
            outbox[1, at, :] = f

    def prepare(k):
        at = rows(k)

        def step(t, carry):
            a, b = carry
            i = jnp.where(is_left, height - 1 - t, t)
            r = r_v[i, at, :]
            a = g_v[i, at, :] + r * a
            b = r * b
            g_v[i, at, :] = a
            r_v[i, at, :] = b
            return a, b

        first = jnp.where(is_left, height - 1, 0)
        lax.fori_loop(1, height, step, (g_v[first, at, :], r_v[first, at, :]), unroll=True)

    def substitute(k):
        at = rows(k)

        @pl.when(is_left)
        def _():
            u = ubox[at, :]
            put(out_ref, height - 1, k, u)

            def step(i, carry):
                put(out_ref, i - 1, k, g_v[i, at, :] + r_v[i, at, :] * u)
                return carry

            lax.fori_loop(1, height, step, 0, unroll=True)

        @pl.when(is_right)
        def _():
            u = ubox[at, :]

            def step(i, carry):
                put(out_ref, i, k, g_v[i, at, :] + r_v[i, at, :] * u)
                return carry

            lax.fori_loop(0, height, step, 0, unroll=True)

    for k in range(count - 1):
        make_source(k)
    face_load.wait()
    greeted = (
        jnp.where(p > 0, 1, 0) + jnp.where(p < gx_size - 1, 1, 0)
        + jnp.where(has_down, 1, 0) + jnp.where(has_up, 1, 0)
    )

    @pl.when(is_end)
    def _():
        eliminate(0)

    pl.semaphore_wait(barrier, greeted)

    @pl.when(has_down)
    def _():
        to_down.start()

    @pl.when(has_up)
    def _():
        to_up.start()

    for k in range(count):
        if k == count - 1:
            @pl.when(has_down)
            def _():
                to_up.wait_recv()

            @pl.when(has_up)
            def _():
                to_down.wait_recv()

            for i in range(height):
                e_v[i, PAD - 1:PAD, :] = halo[0, i:i + 1, :]
                e_v[i, PAD + width:PAD + width + 1, :] = halo[1, i:i + 1, :]
            make_source(k)

        @pl.when(not_end)
        def _():
            message(0, k).wait_recv()
            if k == 0:
                eliminate(k)

        if k > 0:
            eliminate(k)
        message(slot, k).start()

    for k in range(count):
        prepare(k)

    last = jnp.where(is_left, 0, height - 1)
    for k in range(count):
        at = rows(k)

        @pl.when(is_mid)
        def _():
            message(1, k).wait_recv()
            ubox[at, :] = (outbox[1, at, :] + inbox[1, 1, at, :]) / (outbox[0, at, :] + inbox[1, 0, at, :])

        @pl.when(not_mid)
        def _():
            reply(k).wait_recv()

        @pl.when(not_end)
        def _():
            usend[at, :] = g_v[last, at, :] + r_v[last, at, :] * ubox[at, :]
            reply(k).start()

        substitute(k)

    for k in range(count):
        message(slot, k).wait_send()

        @pl.when(not_end)
        def _():
            reply(k).wait_send()

    @pl.when(has_down)
    def _():
        to_down.wait_send()

    @pl.when(has_up)
    def _():
        to_up.wait_send()


def body(energy, coupling):
    height, width, depth = energy.shape
    gx_size, gy_size = lax.axis_size("gx"), lax.axis_size("gy")
    count = len(chunk_list(width))
    f32 = jnp.float32
    block = pltpu.VMEM((height, width, depth), f32)
    plane = pltpu.VMEM((width, depth), f32)
    dma = pltpu.SemaphoreType.DMA
    return pl.pallas_call(
        functools.partial(kernel, gx_size, gy_size),
        out_shape=jax.ShapeDtypeStruct(energy.shape, f32),
        in_specs=[pl.BlockSpec(memory_space=pl.ANY)] * 2,
        out_specs=pl.BlockSpec(memory_space=pltpu.VMEM),
        scratch_shapes=[
            pltpu.VMEM((height, width + 2 * PAD, depth), f32),
            block, block, block, block,
            pltpu.VMEM((2, height, depth), f32),
            pltpu.VMEM((2, height, depth), f32),
            pltpu.VMEM((2, width, depth), f32),
            pltpu.VMEM((2, 2, width, depth), f32),
            plane, plane,
            dma, dma, dma((2,)), dma((2,)),
            dma((count,)), dma((2, count)), dma((count,)), dma((count,)),
        ],
        compiler_params=pltpu.CompilerParams(
            collective_id=0, has_side_effects=True, vmem_limit_bytes=VMEM_LIMIT
        ),
        cost_estimate=pl.CostEstimate(
            flops=30 * height * width * depth, bytes_accessed=12 * height * width * depth, transcendentals=0
        ),
    )(energy, coupling)


def solution(mesh):
    spec = P("gx", "gy", None)
    return jax.shard_map(body, mesh=mesh, in_specs=(spec, spec), out_specs=spec, check_vma=False)
```

```python
import functools

import jax
import jax.numpy as jnp
from jax import lax
from jax.experimental import pallas as pl
from jax.experimental.pallas import tpu as pltpu
from jax.sharding import PartitionSpec as P

Y_WEIGHT = 0.15
PIECES = 7
PAD = 8
VMEM_LIMIT = 52 * 1024 * 1024
MESH = pl.DeviceIdType.MESH


def chunk_list(width):
    tiles = width // PAD - 2
    cuts = [2 * PAD + PAD * (tiles * n // PIECES) for n in range(PIECES + 1)]
    return [(a, b - a) for a, b in zip(cuts, cuts[1:])] + [(0, 2 * PAD)]


def kernel(
    gx_size, gy_size, energy_ref, coupling_ref, out_ref,
    e_v, c_v, b_v, r_v, g_v, edge, halo, outbox, inbox, usend, ubox,
    load_sem, face_sem, halo_send, halo_recv, msg_send, msg_recv, u_send, u_recv,
):
    height, width, _ = energy_ref.shape
    chunks = chunk_list(width)
    count = len(chunks)
    p, q = lax.axis_index("gx"), lax.axis_index("gy")
    half = gx_size // 2
    is_left = p < half
    is_right = p >= half
    is_end = (p == 0) | (p == gx_size - 1)
    is_mid = (p == half - 1) | (p == half)
    not_end = jnp.logical_not(is_end)
    not_mid = jnp.logical_not(is_mid)
    inward = jnp.where(is_left, p + 1, p - 1)
    outward = jnp.where(is_left, p - 1, p + 1)
    slot = jnp.where(is_mid, 1, 0)
    has_down, has_up = q > 0, q < gy_size - 1

    def segments(k):
        start, size = chunks[k]
        if start == 0:
            return [(0, width - PAD, PAD), (PAD, 0, PAD)]
        return [(0, start - PAD, size)]

    def take(ref, i, k, shift=0):
        parts = [ref[i, line + shift:line + shift + n, :] for _, line, n in segments(k)]
        return parts[0] if len(parts) == 1 else jnp.concatenate(parts, axis=0)

    def put(ref, i, k, value):
        for at, line, n in segments(k):
            ref[i, line:line + n, :] = value[at:at + n]

    def rows(k):
        start, size = chunks[k]
        return slice(start, start + size)

    barrier = pltpu.get_barrier_semaphore()

    def greet(cond, device):
        @pl.when(cond)
        def _():
            pl.semaphore_signal(barrier, inc=1, device_id=device, device_id_type=MESH)

    greet(p > 0, (p - 1, q))
    greet(p < gx_size - 1, (p + 1, q))
    greet(has_down, (p, q - 1))
    greet(has_up, (p, q + 1))

    load = pltpu.make_async_copy(energy_ref, e_v.at[:, PAD:PAD + width, :], load_sem)
    load.start()
    face_load = pltpu.make_async_copy(coupling_ref, c_v, face_sem)
    face_load.start()

    @pl.when(is_end)
    def _():
        inbox[0] = jnp.zeros_like(inbox[0])

    load.wait()
    for i in range(height):
        edge[0, i:i + 1, :] = e_v[i, PAD:PAD + 1, :]
        edge[1, i:i + 1, :] = e_v[i, PAD + width - 1:PAD + width, :]

    @pl.when(jnp.logical_not(has_down))
    def _():
        halo[0] = jnp.zeros_like(halo[0])

    @pl.when(jnp.logical_not(has_up))
    def _():
        halo[1] = jnp.zeros_like(halo[1])

    def halo_copy(side, device):
        return pltpu.make_async_remote_copy(
            src_ref=edge.at[side], dst_ref=halo.at[1 - side],
            send_sem=halo_send.at[side], recv_sem=halo_recv.at[1 - side],
            device_id=device, device_id_type=MESH,
        )

    to_down = halo_copy(0, (p, q - 1))
    to_up = halo_copy(1, (p, q + 1))

    def make_source(k):
        def row(i, carry):
            here, before, after = take(e_v, i, k, PAD), take(e_v, i, k, PAD - 1), take(e_v, i, k, PAD + 1)
            b_v[i, rows(k), :] = here + Y_WEIGHT * (before - 2.0 * here + after)
            return carry

        lax.fori_loop(0, height, row, 0, unroll=True)

    def message(s, k):
        return pltpu.make_async_remote_copy(
            src_ref=outbox.at[:, rows(k), :], dst_ref=inbox.at[s, :, rows(k), :],
            send_sem=msg_send.at[k], recv_sem=msg_recv.at[s, k],
            device_id=(inward, q), device_id_type=MESH,
        )

    def reply(k):
        return pltpu.make_async_remote_copy(
            src_ref=usend.at[rows(k)], dst_ref=ubox.at[rows(k)],
            send_sem=u_send.at[k], recv_sem=u_recv.at[k],
            device_id=(outward, q), device_id_type=MESH,
        )

    def eliminate(k):
        at = rows(k)

        @pl.when(is_left)
        def _():
            def step(i, carry):
                e, f = carry
                c = take(c_v, i, k)
                g = pl.reciprocal(c + e)
                r = c * g
                r_v[i, at, :] = r
                g_v[i, at, :] = g * f
                through = r * e
                if isinstance(i, int):
                    through = jnp.where(p == 0, c, through)
                return 1.0 + through, b_v[i, at, :] + r * f

            carry = step(0, (inbox[0, 0, at, :], inbox[0, 1, at, :]))
            e, f = lax.fori_loop(1, height, step, carry, unroll=True)
            outbox[0, at, :] = e
            outbox[1, at, :] = f

        @pl.when(is_right)
        def _():
            def step(t, carry):
                e, f = carry
                i = height - 1 - t
                e = 1.0 + e
                f = b_v[i, at, :] + f
                c = take(c_v, i, k)
                g = pl.reciprocal(c + e)
                r = c * g
                r_v[i, at, :] = r
                g_v[i, at, :] = g * f
                return r * e, r * f

            carry = (inbox[0, 0, at, :], inbox[0, 1, at, :])
            e, f = lax.fori_loop(0, height, step, carry, unroll=True)
            outbox[0, at, :] = e
            outbox[1, at, :] = f

    def prepare(k):
        at = rows(k)

        def step(t, carry):
            a, b = carry
            i = jnp.where(is_left, height - 1 - t, t)
            r = r_v[i, at, :]
            a = g_v[i, at, :] + r * a
            b = r * b
            g_v[i, at, :] = a
            r_v[i, at, :] = b
            return a, b

        first = jnp.where(is_left, height - 1, 0)
        lax.fori_loop(1, height, step, (g_v[first, at, :], r_v[first, at, :]), unroll=True)

    def substitute(k):
        at = rows(k)

        @pl.when(is_left)
        def _():
            u = ubox[at, :]
            put(out_ref, height - 1, k, u)

            def step(i, carry):
                put(out_ref, i - 1, k, g_v[i, at, :] + r_v[i, at, :] * u)
                return carry

            lax.fori_loop(1, height, step, 0, unroll=True)

        @pl.when(is_right)
        def _():
            u = ubox[at, :]

            def step(i, carry):
                put(out_ref, i, k, g_v[i, at, :] + r_v[i, at, :] * u)
                return carry

            lax.fori_loop(0, height, step, 0, unroll=True)

    for k in range(count - 1):
        make_source(k)
    face_load.wait()
    greeted = (
        jnp.where(p > 0, 1, 0) + jnp.where(p < gx_size - 1, 1, 0)
        + jnp.where(has_down, 1, 0) + jnp.where(has_up, 1, 0)
    )

    @pl.when(is_end)
    def _():
        eliminate(0)

    pl.semaphore_wait(barrier, greeted)

    @pl.when(has_down)
    def _():
        to_down.start()

    @pl.when(has_up)
    def _():
        to_up.start()

    for k in range(count):
        if k == count - 1:
            @pl.when(has_down)
            def _():
                to_up.wait_recv()

            @pl.when(has_up)
            def _():
                to_down.wait_recv()

            for i in range(height):
                e_v[i, PAD - 1:PAD, :] = halo[0, i:i + 1, :]
                e_v[i, PAD + width:PAD + width + 1, :] = halo[1, i:i + 1, :]
            make_source(k)

        @pl.when(not_end)
        def _():
            message(0, k).wait_recv()
            if k == 0:
                eliminate(k)

        if k > 0:
            eliminate(k)
        message(slot, k).start()

    for k in range(count):
        prepare(k)

    last = jnp.where(is_left, 0, height - 1)
    for k in range(count):
        at = rows(k)

        @pl.when(is_mid)
        def _():
            message(1, k).wait_recv()
            ubox[at, :] = (outbox[1, at, :] + inbox[1, 1, at, :]) / (outbox[0, at, :] + inbox[1, 0, at, :])

        @pl.when(not_mid)
        def _():
            reply(k).wait_recv()

        @pl.when(not_end)
        def _():
            usend[at, :] = g_v[last, at, :] + r_v[last, at, :] * ubox[at, :]
            reply(k).start()

        @pl.when(not_mid)
        def _():
            substitute(k)

    @pl.when(is_mid)
    def _():
        for k in range(count):
            substitute(k)

    for k in range(count):
        message(slot, k).wait_send()

        @pl.when(not_end)
        def _():
            reply(k).wait_send()

    @pl.when(has_down)
    def _():
        to_down.wait_send()

    @pl.when(has_up)
    def _():
        to_up.wait_send()


def body(energy, coupling):
    height, width, depth = energy.shape
    gx_size, gy_size = lax.axis_size("gx"), lax.axis_size("gy")
    count = len(chunk_list(width))
    f32 = jnp.float32
    block = pltpu.VMEM((height, width, depth), f32)
    plane = pltpu.VMEM((width, depth), f32)
    dma = pltpu.SemaphoreType.DMA
    return pl.pallas_call(
        functools.partial(kernel, gx_size, gy_size),
        out_shape=jax.ShapeDtypeStruct(energy.shape, f32),
        in_specs=[pl.BlockSpec(memory_space=pl.ANY)] * 2,
        out_specs=pl.BlockSpec(memory_space=pltpu.VMEM),
        scratch_shapes=[
            pltpu.VMEM((height, width + 2 * PAD, depth), f32),
            block, block, block, block,
            pltpu.VMEM((2, height, depth), f32),
            pltpu.VMEM((2, height, depth), f32),
            pltpu.VMEM((2, width, depth), f32),
            pltpu.VMEM((2, 2, width, depth), f32),
            plane, plane,
            dma, dma, dma((2,)), dma((2,)),
            dma((count,)), dma((2, count)), dma((count,)), dma((count,)),
        ],
        compiler_params=pltpu.CompilerParams(
            collective_id=0, has_side_effects=True, vmem_limit_bytes=VMEM_LIMIT
        ),
        cost_estimate=pl.CostEstimate(
            flops=30 * height * width * depth, bytes_accessed=12 * height * width * depth, transcendentals=0
        ),
    )(energy, coupling)


def solution(mesh):
    spec = P("gx", "gy", None)
    return jax.shard_map(body, mesh=mesh, in_specs=(spec, spec), out_specs=spec, check_vma=False)
```
